32 devices in a mesh: seq: 8 (over y, x, core), tp: 4 (over z).
Axes of the slice: x: 2, y: 2, z: 4, core: 2. Of those that a mesh axis runs over, the one named last changes fastest.
Arguments:
- embeddings: bfloat16 [3072, 4096], P('seq', 'tp'), may hold values from -6 to 6
- span_mask: int32 [3072], P('seq'), may hold values from 0 to 1, as said below
- sentinel_id: int32 [3072], P('seq'), may hold values from 0 to 99, as said below
- sentinel_table: bfloat16 [100, 4096], P(None, 'tp'), may hold values from -6 to 6
- gen_weight: bfloat16 [4096, 240], P(None, 'tp'), may hold values from -0.1875 to 0.1875
- up_weight: bfloat16 [4096, 8192], P(None, 'tp'), may hold values from -0.09375 to 0.09375
- down_weight: bfloat16 [8192, 4096], P('tp'), may hold values from -0.0625 to 0.0625
- cotangent: bfloat16 [3072, 4096], P('seq', 'tp'), may hold values from -0.59765625 to 0.59765625
Outputs:
- layer_output: bfloat16 [3072, 4096], P('seq', 'tp')
- embed_grad: float32 [3072, 4096], P('seq', 'tp')
- table_grad: float32 [100, 4096], P(None, 'tp')
- gen_grad: float32 [4096, 240], P(None, 'tp')
- up_grad: float32 [4096, 8192], P('seq', 'tp')
- down_grad: float32 [8192, 4096], P('tp', 'seq')
The draws below stay inside these ranges and needn't reach their ends.
Inputs may be any that keep to these rules, and one draw needn't show every extreme that they name: `span_mask`: the tokens fall into aligned blocks of 16; each block holds exactly one span of 1 to 3 consecutive tokens marked 1, the rest 0. `sentinel_id`: all 16 tokens of an aligned block carry the same sentinel id.
All inputs are finite; a program needn't handle non-finite values.
Results may differ from the reference program's by a relative error of at most 0.035.
Values may be sent and summed in bfloat16 or wider, within the bound.
A program may use at most 192 MiB of HBM per device.

```python
import jax
import jax.numpy as jnp
from jax import lax

D = 4096
FF = 8192
HEADS = 16
KW = 15
SENT = 100
TOK_DEV = 384
LENGTH = 3072
N_SEQ = 8
N_TP = 4


def span_layout(key):
    blocks = LENGTH // 16
    key_start, key_length, key_ids, key_top = jax.random.split(jax.random.fold_in(key, 11), 4)
    span_start = jax.random.randint(key_start, (blocks,), 0, 14)
    span_length = jax.random.randint(key_length, (blocks,), 1, 4)
    block_ids = jax.random.randint(key_ids, (blocks,), 0, SENT)
    top_block = jax.random.randint(key_top, (), 0, blocks)
    block_ids = jnp.where(jnp.arange(blocks) == top_block, SENT - 1, block_ids)
    offset = jnp.arange(16)[None, :]
    inside = (offset >= span_start[:, None]) & (offset < span_start[:, None] + span_length[:, None])
    span_mask = inside.astype(jnp.int32).reshape(-1)
    sentinel = jnp.broadcast_to(block_ids[:, None], (blocks, 16)).reshape(-1).astype(jnp.int32)
    return (span_mask, sentinel)


def draw_span_mask(key, part):
    return span_layout(key)[0]


def draw_sentinel_id(key, part):
    return span_layout(key)[1]


def raised(array, stream_key, source, target, parts, factor):
    def block_of(axis_at):
        return (jnp.arange(array.shape[axis_at]) // (array.shape[axis_at] // parts)).reshape((-1,) + (1,) * (array.ndim - 1 - axis_at))

    near = jax.random.permutation(stream_key, parts)[block_of(target)]
    other_side = (block_of(target) + parts // 2) % parts
    return jnp.where((block_of(source) == near) | (block_of(source) == other_side), factor * array, array)


def shard_levels(rng, shape, shards, smallest, high):
    level, own = 1.0, jax.random.fold_in(rng, 6)
    for axis_at, shards_of in shards:
        heights = jnp.exp(jax.random.uniform(jax.random.fold_in(own, axis_at), (shards_of,), jnp.float32, smallest / len(shards), high / len(shards)))
        level = level * jnp.repeat(heights, shape[axis_at] // shards_of).reshape([-1 if axis == axis_at else 1 for axis in range(len(shape))])
    return level


def noise(own_key, dims, scale, limit, cuts=(), kind=jnp.bfloat16):
    loudness = shard_levels(own_key, dims, cuts, -0.22, 0.18) if cuts else 1.0
    result = jax.random.normal(own_key, dims, jnp.float32) * scale * loudness
    return jnp.minimum(jnp.maximum(result, -limit), limit).astype(kind)


def bell_draw_with(key, dims, deviation, reach, shards, heavy, held_as=jnp.bfloat16):
    result = deviation * jax.random.normal(key, dims, jnp.float32)
    if shards:
        result = result * shard_levels(key, dims, shards, -0.22, 0.18)
    return jnp.clip(raised(result, jax.random.fold_in(key, 3), *heavy), -reach, reach).astype(held_as)


def setup_inputs(seed: int = 0) -> dict:
    key_of = jax.random.split(jax.random.key(seed), 9)
    return {
        "embeddings": noise(key_of[0], (LENGTH, D), 1.0, 6.0, ((0, 8), (1, 4))),
        "span_mask": draw_span_mask(jax.random.fold_in(key_of[8], 71), 0),
        "sentinel_id": draw_sentinel_id(jax.random.fold_in(key_of[8], 71), 0),
        "sentinel_table": noise(key_of[3], (SENT, D), 1.0, 6.0, ((1, 4),)),
        "gen_weight": noise(key_of[4], (D, HEADS * KW), (D // 4) ** -0.5, 0.1875, ((1, 4),)),
        "up_weight": noise(key_of[5], (D, FF), D ** -0.5, 0.09375, ((1, 4),)),
        "down_weight": noise(key_of[6], (FF, D), FF ** -0.5, 0.0625, ((0, 4),)),
        "cotangent": bell_draw_with(key_of[7], (LENGTH, D), 0.1, 0.59765625, ((0, 8), (1, 4)), (0, 1, 8, 2.0)),
    }


def gelu_tanh(values):
    return jax.nn.gelu(values, approximate=True)

def rounded(values):
    return lax.optimization_barrier(values.astype(jnp.bfloat16)).astype(jnp.float32)

def reference(embeddings, span_mask, sentinel_id, sentinel_table, gen_weight, up_weight, down_weight, cotangent):
    tap_reach = (KW - 1) // 2
    head_width = D // HEADS
    onehot = sentinel_id[:, None] == jnp.arange(SENT, dtype=jnp.int32)[None, :]
    picked = jnp.dot(onehot.astype(jnp.bfloat16), sentinel_table, preferred_element_type=jnp.float32).astype(jnp.bfloat16)
    masked = span_mask[:, None] == 1
    hidden = jnp.where(masked, picked, embeddings)
    logits = jnp.dot(hidden, gen_weight, preferred_element_type=jnp.float32)
    exp_logits = jnp.exp(logits.reshape(LENGTH, HEADS, KW))
    kernel = exp_logits / lax.optimization_barrier(jnp.sum(exp_logits, axis=-1, keepdims=True))
    padded = jnp.pad(hidden, ((tap_reach, tap_reach), (0, 0))).reshape(LENGTH + 2 * tap_reach, HEADS, head_width).astype(jnp.float32)
    conv_sum = jnp.zeros((LENGTH, HEADS, head_width), jnp.float32)
    for tap_index in range(KW):
        conv_sum = conv_sum + kernel[:, :, tap_index, None] * padded[tap_index:tap_index + LENGTH]
    act = (hidden.astype(jnp.float32) + conv_sum.reshape(LENGTH, D)).astype(jnp.bfloat16)
    pre_act = jnp.dot(act, up_weight, preferred_element_type=jnp.float32)
    middle, gelu_back = jax.vjp(gelu_tanh, pre_act)
    middle = middle.astype(jnp.bfloat16)
    block_size = FF // N_TP
    ffn_total = jnp.zeros((LENGTH, D), jnp.float32)
    for group_index in range(N_TP):
        lower = group_index * block_size
        ffn_total = ffn_total + rounded(jnp.dot(middle[:, lower:lower + block_size], down_weight[lower:lower + block_size], preferred_element_type=jnp.float32))
    layer_output = (act.astype(jnp.float32) + ffn_total).astype(jnp.bfloat16)
    middle_grad = jnp.dot(cotangent, down_weight.T, preferred_element_type=jnp.float32)
    pre_grad = gelu_back(middle_grad)[0].astype(jnp.bfloat16)
    down_grad = jnp.zeros((FF, D), jnp.float32)
    up_grad = jnp.zeros((D, FF), jnp.float32)
    for group_index in range(N_SEQ):
        lower = group_index * TOK_DEV
        down_grad = down_grad + rounded(jnp.dot(middle[lower:lower + TOK_DEV].T, cotangent[lower:lower + TOK_DEV], preferred_element_type=jnp.float32))
        up_grad = up_grad + rounded(jnp.dot(act[lower:lower + TOK_DEV].T, pre_grad[lower:lower + TOK_DEV], preferred_element_type=jnp.float32))
    act_grad = cotangent.astype(jnp.float32)
    for group_index in range(N_TP):
        lower = group_index * block_size
        act_grad = act_grad + rounded(jnp.dot(pre_grad[:, lower:lower + block_size], up_weight[:, lower:lower + block_size].T, preferred_element_type=jnp.float32))
    act_three = act_grad.reshape(LENGTH, HEADS, head_width)
    kernel_grad = jnp.stack([lax.optimization_barrier(jnp.sum(act_three * padded[tap_index:tap_index + LENGTH], axis=-1)) for tap_index in range(KW)], axis=-1)
    weighted = lax.optimization_barrier(jnp.sum(kernel * kernel_grad, axis=-1, keepdims=True))
    logit_grad = (kernel * (kernel_grad - weighted)).reshape(LENGTH, HEADS * KW).astype(jnp.bfloat16)
    gen_grad = jnp.dot(hidden.T, logit_grad, preferred_element_type=jnp.float32)
    grad_pad = jnp.pad(act_three, ((tap_reach, tap_reach), (0, 0), (0, 0)))
    kernel_pad = jnp.pad(kernel, ((tap_reach, tap_reach), (0, 0), (0, 0)))
    conv_back = jnp.zeros((LENGTH, HEADS, head_width), jnp.float32)
    for tap_index in range(KW):
        lower = 2 * tap_reach - tap_index
        conv_back = conv_back + kernel_pad[lower:lower + LENGTH, :, tap_index, None] * grad_pad[lower:lower + LENGTH]
    hidden_grad = act_grad + conv_back.reshape(LENGTH, D) + jnp.dot(logit_grad, gen_weight.T, preferred_element_type=jnp.float32)
    embed_grad = jnp.where(masked, jnp.float32(0.0), hidden_grad)
    table_grad = jnp.dot(onehot.astype(jnp.float32).T, jnp.where(masked, hidden_grad, jnp.float32(0.0)), precision=lax.Precision.HIGHEST)
    return (layer_output, embed_grad, table_grad, gen_grad, up_grad, down_grad)
```

```python
import jax
import jax.numpy as jnp
from jax import lax
from jax.sharding import PartitionSpec as P

KW = 15
SENT = 100


def halo(low_edge, high_edge):
    count = lax.axis_size("seq")
    forward = [(i, i + 1) for i in range(count - 1)]
    backward = [(target, source) for source, target in forward]
    low = lax.ppermute(high_edge, "seq", forward)
    high = lax.ppermute(low_edge, "seq", backward)
    return low, high


def gelu_tanh(values):
    return jax.nn.gelu(values, approximate=True)


def dot(a, b, dims=((1,), (0,))):
    return lax.dot_general(a, b, (dims, ((), ())), preferred_element_type=jnp.float32)


def turned(block, shift):
    count = lax.axis_size("tp")
    return lax.ppermute(block, "tp", [(i, (i + shift) % count) for i in range(count)])


def swapped(block, bit):
    count = lax.axis_size("seq")
    return lax.ppermute(block, "seq", [(i, i ^ (1 << bit)) for i in range(count)])


def my_bit(bit):
    return (lax.axis_index("seq") // (1 << bit)) % 2


def scatter_sum(pieces, bits, order):
    bits = list(bits)
    for bit in order:
        axis = bits.index(bit)
        bits.pop(axis)
        mine = my_bit(bit)

        def part(which):
            total = 0.0
            for piece in pieces:
                total = total + lax.dynamic_index_in_dim(
                    piece, which, axis, keepdims=False
                ).astype(jnp.float32)
            return total.astype(jnp.bfloat16)

        pieces = [part(mine), swapped(part(1 - mine), bit)]
    return pieces[0].astype(jnp.float32) + pieces[1].astype(jnp.float32)


def seq_bits():
    return lax.axis_size("seq").bit_length() - 1


def weight_grad(features, factor):
    count, depth = seq_bits(), features.shape[0]
    rows = features.shape[1] >> count
    grouped = features.reshape(depth, 1 << (count - 1), 2, rows)
    width = factor.shape[1]

    def half(which, factor):
        chosen = lax.dynamic_index_in_dim(grouped, which, 2, keepdims=False)
        return dot(chosen.reshape(depth, -1), factor, ((0,), (0,))).astype(jnp.bfloat16)

    mine = my_bit(0)
    sent = half(1 - mine, factor)
    sent, factor = lax.optimization_barrier((sent, factor))
    got = swapped(sent, 0)
    kept = half(mine, factor)
    shape = (2,) * (count - 1) + (2, rows // 2, width)
    bits = list(range(count - 1, 0, -1))
    pieces = [kept.reshape(shape), got.reshape(shape)]
    lead = len(bits)
    upper = scatter_sum([lax.index_in_dim(p, 0, lead, False) for p in pieces], bits, bits)
    lower = scatter_sum([lax.index_in_dim(p, 1, lead, False) for p in pieces], bits, bits[::-1])
    return jnp.concatenate([upper, lower], axis=0)


def seq_sum(values):
    def step(block, bit):
        other = swapped(block, bit)
        return (block.astype(jnp.float32) + other.astype(jnp.float32)).astype(jnp.bfloat16)

    values = step(values, 0)
    cut = values.shape[0] // 2 // 16 * 16
    first, second = values[:cut], values[cut:]
    bits = list(range(1, seq_bits()))
    for one, two in zip(bits, bits[::-1]):
        first, second = step(first, one), step(second, two)
    return jnp.concatenate([first, second], axis=0)


def body(
    embeddings,
    span_mask,
    sentinel_id,
    sentinel_table,
    gen_weight,
    up_weight,
    down_weight,
    cotangent,
):
    bf16, f32 = jnp.bfloat16, jnp.float32
    tok_rows, feat_width = embeddings.shape
    gen_cols = gen_weight.shape[1]
    head_count = gen_cols // KW
    head_width = feat_width // head_count
    reach = (KW - 1) // 2
    tp_count, tp_index = lax.axis_size("tp"), lax.axis_index("tp")
    sentinel_codes = jnp.arange(SENT, dtype=jnp.int32)
    onehot = sentinel_id[:, None] == sentinel_codes[None, :]
    picked = dot(onehot.astype(bf16), sentinel_table).astype(bf16)
    masked = span_mask[:, None] == 1
    hidden = jnp.where(masked, picked, embeddings)

    gen_blocks = []
    for shift in range(tp_count):
        start = (tp_index + shift) % tp_count * feat_width
        rows = lax.dynamic_slice_in_dim(gen_weight, start, feat_width, axis=0)
        gen_blocks.append(turned(rows, shift) if shift else rows)
    gen_rows = jnp.concatenate(gen_blocks, axis=1)
    partial = dot(hidden, gen_rows)
    logits = partial[:, :gen_cols]
    for shift in range(1, tp_count):
        logits = logits + turned(partial[:, shift * gen_cols : (shift + 1) * gen_cols], -shift)
    exp_logits = jnp.exp(logits)
    kernels = []
    for head in range(head_count):
        taps = exp_logits[:, head * KW : (head + 1) * KW]
        kernels.append(taps / jnp.sum(taps, axis=-1, keepdims=True))

    low, high = halo(hidden[:reach], hidden[tok_rows - reach :])
    padded = jnp.concatenate([low, hidden, high], axis=0)
    long_rows = tok_rows + 2 * reach
    ahead = jnp.arange(long_rows)[None, :] - jnp.arange(tok_rows)[:, None]
    conv = []
    for head in range(head_count):
        columns = slice(head * head_width, (head + 1) * head_width)
        band = jnp.zeros((tok_rows, long_rows), f32)
        for tap in range(KW):
            band = jnp.where(ahead == tap, kernels[head][:, tap : tap + 1], band)
        conv.append(dot(band.astype(bf16), padded[:, columns]))
    act = (hidden.astype(f32) + jnp.concatenate(conv, axis=1)).astype(bf16)

    full_cot = lax.all_gather(cotangent, "tp", axis=1, tiled=True)
    full_act = lax.all_gather(act, "tp", axis=1, tiled=True)
    middle_grad = dot(full_cot, down_weight, ((1,), (1,)))
    pre_sum = dot(full_act, up_weight)
    middle, gelu_back = jax.vjp(gelu_tanh, pre_sum)
    middle = middle.astype(bf16)
    pre_grad = gelu_back(middle_grad)[0].astype(bf16)

    back_part = dot(up_weight, pre_grad, ((1,), (1,))).astype(bf16)
    back_part, middle, pre_grad = lax.optimization_barrier((back_part, middle, pre_grad))
    act_back = lax.psum_scatter(back_part, "tp", scatter_dimension=0, tiled=True)
    down_grad = weight_grad(full_cot, middle).T
    up_grad = weight_grad(full_act, pre_grad)
    ffn_part = dot(down_weight, middle, ((0,), (1,))).astype(bf16)
    ffn_total = lax.psum_scatter(ffn_part, "tp", scatter_dimension=0, tiled=True)
    layer_output = (act.astype(f32) + ffn_total.astype(f32).T).astype(bf16)

    act_grad = cotangent.astype(f32) + act_back.astype(f32).T
    short_grad = act_grad.astype(bf16)
    kernel_short = jnp.concatenate(kernels, axis=1).astype(bf16)
    joined = jnp.concatenate([short_grad, kernel_short], axis=1)
    low, high = halo(joined[:reach], joined[tok_rows - reach :])
    grad_pad = jnp.concatenate([low[:, :feat_width], short_grad, high[:, :feat_width]], axis=0)
    kernel_pad = jnp.concatenate([low[:, feat_width:], kernel_short, high[:, feat_width:]], axis=0)
    logit_grads = []
    for head in range(head_count):
        columns = slice(head * head_width, (head + 1) * head_width)
        scores = dot(short_grad[:, columns], padded[:, columns], ((1,), (1,)))
        kernel_grad = jnp.stack(
            [jnp.sum(jnp.where(ahead == tap, scores, 0.0), axis=-1) for tap in range(KW)], axis=-1
        )
        weighted = jnp.sum(kernels[head] * kernel_grad, axis=-1, keepdims=True)
        logit_grads.append((kernels[head] * (kernel_grad - weighted)).astype(bf16))
    logit_grad = jnp.concatenate(logit_grads, axis=1)
    logit_grads = jnp.concatenate(
        [logit_grad] + [turned(logit_grad, shift) for shift in range(1, tp_count)], axis=1
    )

    behind = jnp.arange(tok_rows)[None, :] - jnp.arange(long_rows)[:, None] + 2 * reach
    conv_back = []
    for head in range(head_count):
        columns = slice(head * head_width, (head + 1) * head_width)
        band = jnp.zeros((long_rows, tok_rows), f32)
        for tap in range(KW):
            place = head * KW + tap
            band = jnp.where(behind == tap, kernel_pad[:, place : place + 1].astype(f32), band)
        conv_back.append(dot(band.astype(bf16), grad_pad[:, columns], ((0,), (0,))))

    gen_part = dot(logit_grads, hidden, ((0,), (0,))).astype(bf16)
    gen_owned = [gen_part[:gen_cols]]
    for shift in range(1, tp_count):
        gen_owned.append(turned(gen_part[shift * gen_cols : (shift + 1) * gen_cols], -shift))
    gen_back = dot(logit_grads, gen_rows, ((1,), (1,)))
    hidden_grad = act_grad + jnp.concatenate(conv_back, axis=1) + gen_back
    embed_grad = jnp.where(masked, f32(0.0), hidden_grad)
    table_part = dot(
        onehot.astype(bf16), jnp.where(masked, hidden_grad, f32(0.0)).astype(bf16), ((0,), (0,))
    ).astype(bf16)
    summed = seq_sum(jnp.concatenate(gen_owned + [table_part], axis=0))
    gen_total = tp_count * gen_cols
    table_grad = summed[gen_total:].astype(f32)
    gen_sum = summed[:gen_total].reshape(tp_count, gen_cols, feat_width)
    gen_sum = lax.dynamic_slice_in_dim(
        jnp.concatenate([gen_sum, gen_sum], axis=0), (tp_count - tp_index) % tp_count, tp_count, axis=0
    )
    gen_sum = gen_sum.transpose(0, 2, 1).reshape(tp_count * feat_width, gen_cols).astype(f32)
    return (layer_output, embed_grad, table_grad, gen_sum, up_grad, down_grad)


def solution(mesh):
    placed = (
        P("seq", "tp"),
        P("seq"),
        P("seq"),
        P(None, "tp"),
        P(None, "tp"),
        P(None, "tp"),
        P("tp", None),
        P("seq", "tp"),
    )
    return jax.shard_map(
        body,
        mesh=mesh,
        in_specs=placed,
        out_specs=(
            P("seq", "tp"),
            P("seq", "tp"),
            P(None, "tp"),
            P(None, "tp"),
            P("seq", "tp"),
            P("tp", "seq"),
        ),
        check_vma=False,
    )
```

```python
import jax
import jax.numpy as jnp
from jax import lax
from jax.sharding import PartitionSpec as P

KW = 15
SENT = 100


def halo(low_edge, high_edge):
    count = lax.axis_size("seq")
    forward = [(i, i + 1) for i in range(count - 1)]
    backward = [(target, source) for source, target in forward]
    low = lax.ppermute(high_edge, "seq", forward)
    high = lax.ppermute(low_edge, "seq", backward)
    return low, high


def gelu_tanh(values):
    return jax.nn.gelu(values, approximate=True)


def dot(a, b, dims=((1,), (0,))):
    return lax.dot_general(a, b, (dims, ((), ())), preferred_element_type=jnp.float32)


def turned(block, shift):
    count = lax.axis_size("tp")
    return lax.ppermute(block, "tp", [(i, (i + shift) % count) for i in range(count)])


def swapped(block, bit):
    count = lax.axis_size("seq")
    return lax.ppermute(block, "seq", [(i, i ^ (1 << bit)) for i in range(count)])


def my_bit(bit):
    return (lax.axis_index("seq") // (1 << bit)) % 2


def seq_bits():
    return lax.axis_size("seq").bit_length() - 1


def chosen(pieces, which, axis):
    total = 0.0
    for piece in pieces:
        part = lax.dynamic_index_in_dim(piece, which, axis, keepdims=False)
        total = total + part.astype(jnp.float32)
    return total.astype(jnp.bfloat16)


def first_halves(features, factor):
    count, depth = seq_bits(), features.shape[0]
    rows = features.shape[1] >> count
    grouped = features.reshape(depth, 1 << (count - 1), 2, rows)
    width = factor.shape[1] // 2
    shape = (2,) * (count - 1) + (rows, width)
    mine = my_bit(0)
    other = lax.dynamic_index_in_dim(grouped, 1 - mine, 2, keepdims=False).reshape(depth, -1)
    own = lax.dynamic_index_in_dim(grouped, mine, 2, keepdims=False).reshape(depth, -1)
    sent = []
    for side in range(2):
        columns = factor[:, side * width : (side + 1) * width]
        sent.append(dot(other, columns, ((0,), (0,))).astype(jnp.bfloat16).reshape(shape))

    def kept(factor):
        result = []
        for side in range(2):
            columns = factor[:, side * width : (side + 1) * width]
            result.append(dot(own, columns, ((0,), (0,))).astype(jnp.bfloat16).reshape(shape))
        return result

    return sent, kept


def send_parts(pieces, bits, bit):
    return chosen(pieces, 1 - my_bit(bit), bits.index(bit))


def keep_parts(pieces, bits, bit):
    return chosen(pieces, my_bit(bit), bits.index(bit))


def seq_sum(values):
    def step(block, bit):
        other = swapped(block, bit)
        return (block.astype(jnp.float32) + other.astype(jnp.float32)).astype(jnp.bfloat16)

    values = step(values, 0)
    cut = values.shape[0] // 2 // 16 * 16
    first, second = values[:cut], values[cut:]
    bits = list(range(1, seq_bits()))
    for one, two in zip(bits, bits[::-1]):
        first, second = step(first, one), step(second, two)
    return jnp.concatenate([first, second], axis=0)


def body(
    embeddings,
    span_mask,
    sentinel_id,
    sentinel_table,
    gen_weight,
    up_weight,
    down_weight,
    cotangent,
):
    bf16, f32 = jnp.bfloat16, jnp.float32
    tok_rows, feat_width = embeddings.shape
    gen_cols = gen_weight.shape[1]
    head_count = gen_cols // KW
    head_width = feat_width // head_count
    reach = (KW - 1) // 2
    tp_count, tp_index = lax.axis_size("tp"), lax.axis_index("tp")
    sentinel_codes = jnp.arange(SENT, dtype=jnp.int32)
    onehot = sentinel_id[:, None] == sentinel_codes[None, :]
    picked = dot(onehot.astype(bf16), sentinel_table).astype(bf16)
    masked = span_mask[:, None] == 1
    hidden = jnp.where(masked, picked, embeddings)

    gen_blocks = []
    for shift in range(tp_count):
        start = (tp_index + shift) % tp_count * feat_width
        rows = lax.dynamic_slice_in_dim(gen_weight, start, feat_width, axis=0)
        gen_blocks.append(turned(rows, shift) if shift else rows)
    gen_rows = jnp.concatenate(gen_blocks, axis=1)
    partial = dot(hidden, gen_rows)
    logits = partial[:, :gen_cols]
    for shift in range(1, tp_count):
        logits = logits + turned(partial[:, shift * gen_cols : (shift + 1) * gen_cols], -shift)
    exp_logits = jnp.exp(logits)
    kernels = []
    for head in range(head_count):
        taps = exp_logits[:, head * KW : (head + 1) * KW]
        kernels.append(taps / jnp.sum(taps, axis=-1, keepdims=True))

    low, high = halo(hidden[:reach], hidden[tok_rows - reach :])
    padded = jnp.concatenate([low, hidden, high], axis=0)
    long_rows = tok_rows + 2 * reach
    ahead = jnp.arange(long_rows)[None, :] - jnp.arange(tok_rows)[:, None]
    conv = []
    for head in range(head_count):
        columns = slice(head * head_width, (head + 1) * head_width)
        band = jnp.zeros((tok_rows, long_rows), f32)
        for tap in range(KW):
            band = jnp.where(ahead == tap, kernels[head][:, tap : tap + 1], band)
        conv.append(dot(band.astype(bf16), padded[:, columns]))
    act = (hidden.astype(f32) + jnp.concatenate(conv, axis=1)).astype(bf16)

    full_cot = lax.all_gather(cotangent, "tp", axis=1, tiled=True)
    full_act = lax.all_gather(act, "tp", axis=1, tiled=True)
    middle_grad = dot(full_cot, down_weight, ((1,), (1,)))
    pre_sum = dot(full_act, up_weight)
    middle, gelu_back = jax.vjp(gelu_tanh, pre_sum)
    middle = middle.astype(bf16)
    pre_grad = gelu_back(middle_grad)[0].astype(bf16)

    back_part = dot(up_weight, pre_grad, ((1,), (1,))).astype(bf16)
    back_part, middle, pre_grad = lax.optimization_barrier((back_part, middle, pre_grad))
    act_back = lax.psum_scatter(back_part, "tp", scatter_dimension=0, tiled=True)
    down_sent, down_kept = first_halves(full_cot, middle)
    up_sent, up_kept = first_halves(full_act, pre_grad)
    down_sent, up_sent, middle, pre_grad = lax.optimization_barrier(
        (down_sent, up_sent, middle, pre_grad)
    )
    got = [swapped(block, 0) for block in down_sent + up_sent]
    kept = down_kept(middle) + up_kept(pre_grad)
    kept, middle = lax.optimization_barrier((kept, middle))
    ffn_part = dot(down_weight, middle, ((0,), (1,))).astype(bf16)
    ffn_total = lax.psum_scatter(ffn_part, "tp", scatter_dimension=0, tiled=True)
    high_bits = list(range(seq_bits() - 1, 0, -1))
    orders = [high_bits, high_bits[::-1]] * 2
    lines = [[one, two] for one, two in zip(kept, got)]
    left = [list(high_bits) for _ in lines]

    def send_all(which, step):
        return [send_parts(lines[i], left[i], orders[i][step]) for i in which]

    def swap_all(which, step, sent):
        return [swapped(block, orders[i][step]) for i, block in zip(which, sent)]

    def join_all(which, step, got):
        for i, block in zip(which, got):
            lines[i] = [keep_parts(lines[i], left[i], orders[i][step]), block]
            left[i].remove(orders[i][step])

    downs, ups = (0, 1), (2, 3)
    down_sent, up_sent = send_all(downs, 0), send_all(ups, 0)
    act_back, down_sent, up_sent = lax.optimization_barrier((act_back, down_sent, up_sent))
    down_got, up_got = swap_all(downs, 0, down_sent), swap_all(ups, 0, up_sent)
    layer_output = (act.astype(f32) + ffn_total.astype(f32).T).astype(bf16)

    act_grad = cotangent.astype(f32) + act_back.astype(f32).T
    short_grad = act_grad.astype(bf16)
    kernel_short = jnp.concatenate(kernels, axis=1).astype(bf16)
    low, high = halo(
        jnp.concatenate([short_grad[:reach], kernel_short[:reach]], axis=1),
        jnp.concatenate([short_grad[tok_rows - reach :], kernel_short[tok_rows - reach :]], axis=1),
    )
    grad_pad = jnp.concatenate([low[:, :feat_width], short_grad, high[:, :feat_width]], axis=0)
    kernel_pad = jnp.concatenate([low[:, feat_width:], kernel_short, high[:, feat_width:]], axis=0)
    taps_at = jnp.arange(gen_cols)
    kernel_grad = jnp.zeros((tok_rows, gen_cols), f32)
    for head in range(head_count):
        columns = slice(head * head_width, (head + 1) * head_width)
        scores = dot(short_grad[:, columns], padded[:, columns], ((1,), (1,)))
        for tap in range(KW):
            one = jnp.sum(jnp.where(ahead == tap, scores, 0.0), axis=-1, keepdims=True)
            kernel_grad = jnp.where(taps_at[None, :] == head * KW + tap, one, kernel_grad)
    kernel = jnp.concatenate(kernels, axis=1)
    same_head = (taps_at[:, None] // KW == taps_at[None, :] // KW).astype(f32)
    weighted = jnp.dot(kernel * kernel_grad, same_head, precision=lax.Precision.HIGHEST)
    logit_grad = (kernel * (kernel_grad - weighted)).astype(bf16)
    logit_grad, down_got = lax.optimization_barrier((logit_grad, down_got))
    join_all(downs, 0, down_got)
    down_sent = send_all(downs, 1)
    logit_grads = jnp.concatenate(
        [logit_grad] + [turned(logit_grad, shift) for shift in range(1, tp_count)], axis=1
    )

    logit_grads, up_got = lax.optimization_barrier((logit_grads, up_got))

    behind = jnp.arange(tok_rows)[None, :] - jnp.arange(long_rows)[:, None] + 2 * reach
    conv_back = []
    for head in range(head_count):
        columns = slice(head * head_width, (head + 1) * head_width)
        band = jnp.zeros((long_rows, tok_rows), f32)
        for tap in range(KW):
            place = head * KW + tap
            band = jnp.where(behind == tap, kernel_pad[:, place : place + 1].astype(f32), band)
        conv_back.append(dot(band.astype(bf16), grad_pad[:, columns], ((0,), (0,))))

    gen_part = dot(logit_grads, hidden, ((0,), (0,))).astype(bf16)
    gen_owned = [gen_part[:gen_cols]]
    for shift in range(1, tp_count):
        gen_owned.append(turned(gen_part[shift * gen_cols : (shift + 1) * gen_cols], -shift))
    gen_back = dot(logit_grads, gen_rows, ((1,), (1,)))
    hidden_grad = act_grad + jnp.concatenate(conv_back, axis=1) + gen_back
    embed_grad = jnp.where(masked, f32(0.0), hidden_grad)
    table_part = dot(
        onehot.astype(bf16), jnp.where(masked, hidden_grad, f32(0.0)).astype(bf16), ((0,), (0,))
    ).astype(bf16)
    sums = jnp.concatenate(gen_owned + [table_part], axis=0)
    join_all(ups, 0, up_got)
    up_sent = send_all(ups, 1)
    down_got = swap_all(downs, 1, down_sent)
    sums, up_sent, down_got = lax.optimization_barrier((sums, up_sent, down_got))
    up_got = swap_all(ups, 1, up_sent)
    join_all(downs, 1, down_got)
    join_all(ups, 1, up_got)
    for step in range(2, len(high_bits)):
        join_all(range(4), step, swap_all(range(4), step, send_all(range(4), step)))
    ends = [one.astype(f32) + two.astype(f32) for one, two in lines]
    down_grad = jnp.concatenate(ends[:2], axis=1).T
    up_grad = jnp.concatenate(ends[2:], axis=1)
    summed = seq_sum(sums)
    gen_total = tp_count * gen_cols
    table_grad = summed[gen_total:].astype(f32)
    gen_sum = summed[:gen_total].reshape(tp_count, gen_cols, feat_width)
    gen_sum = lax.dynamic_slice_in_dim(
        jnp.concatenate([gen_sum, gen_sum], axis=0), (tp_count - tp_index) % tp_count, tp_count, axis=0
    )
    gen_sum = gen_sum.transpose(0, 2, 1).reshape(tp_count * feat_width, gen_cols).astype(f32)
    return (layer_output, embed_grad, table_grad, gen_sum, up_grad, down_grad)


def solution(mesh):
    placed = (
        P("seq", "tp"),
        P("seq"),
        P("seq"),
        P(None, "tp"),
        P(None, "tp"),
        P(None, "tp"),
        P("tp", None),
        P("seq", "tp"),
    )
    return jax.shard_map(
        body,
        mesh=mesh,
        in_specs=placed,
        out_specs=(
            P("seq", "tp"),
            P("seq", "tp"),
            P(None, "tp"),
            P(None, "tp"),
            P("seq", "tp"),
            P("tp", "seq"),
        ),
        check_vma=False,
    )
```

```python
import jax
import jax.numpy as jnp
from jax import lax
from jax.experimental.layout import Layout, with_layout_constraint
from jax.sharding import PartitionSpec as P

KW = 15
SENT = 100


def halo(low_edge, high_edge):
    count = lax.axis_size("seq")
    forward = [(i, i + 1) for i in range(count - 1)]
    backward = [(target, source) for source, target in forward]
    low = lax.ppermute(high_edge, "seq", forward)
    high = lax.ppermute(low_edge, "seq", backward)
    return low, high


def gelu_tanh(values):
    return jax.nn.gelu(values, approximate=True)


def dot(a, b, dims=((1,), (0,))):
    return lax.dot_general(a, b, (dims, ((), ())), preferred_element_type=jnp.float32)


def turned(block, shift):
    count = lax.axis_size("tp")
    return lax.ppermute(block, "tp", [(i, (i + shift) % count) for i in range(count)])


def swapped(block, bit):
    count = lax.axis_size("seq")
    return lax.ppermute(block, "seq", [(i, i ^ (1 << bit)) for i in range(count)])


def my_bit(bit):
    return (lax.axis_index("seq") // (1 << bit)) % 2


def row_major(block):
    return with_layout_constraint(block, Layout(major_to_minor=(0, 1)))


def seq_bits():
    return lax.axis_size("seq").bit_length() - 1


def chosen(pieces, which, axis):
    total = 0.0
    for piece in pieces:
        part = lax.dynamic_index_in_dim(piece, which, axis, keepdims=False)
        total = total + part.astype(jnp.float32)
    return total.astype(jnp.bfloat16)


def first_halves(features, factor):
    count = seq_bits()
    rows = features.shape[1] >> count
    width = factor.shape[1] // 2
    shape = (2,) * (count - 1) + (rows, width)
    mine = my_bit(0)

    def blocks(which):
        result = []
        for pair in range(0, 1 << count, 2):
            low = features[:, pair * rows : (pair + 1) * rows]
            high = features[:, (pair + 1) * rows : (pair + 2) * rows]
            result.append(jnp.where(which == 0, low, high))
        return jnp.concatenate(result, axis=1)

    other, own = blocks(1 - mine), blocks(mine)
    sent = []
    for side in range(2):
        columns = factor[:, side * width : (side + 1) * width]
        sent.append(dot(other, columns, ((0,), (0,))).astype(jnp.bfloat16).reshape(shape))

    def kept(factor):
        result = []
        for side in range(2):
            columns = factor[:, side * width : (side + 1) * width]
            result.append(dot(own, columns, ((0,), (0,))).astype(jnp.bfloat16).reshape(shape))
        return result

    return sent, kept


def send_parts(pieces, bits, bit):
    return chosen(pieces, 1 - my_bit(bit), bits.index(bit))


def keep_parts(pieces, bits, bit):
    return chosen(pieces, my_bit(bit), bits.index(bit))


def seq_sum(values):
    def step(block, bit):
        other = swapped(block, bit)
        return (block.astype(jnp.float32) + other.astype(jnp.float32)).astype(jnp.bfloat16)

    values = step(values, 0)
    cut = values.shape[0] // 2 // 16 * 16
    first, second = values[:cut], values[cut:]
    bits = list(range(1, seq_bits()))
    for one, two in zip(bits, bits[::-1]):
        first, second = step(first, one), step(second, two)
    return jnp.concatenate([first, second], axis=0)


def body(
    embeddings,
    span_mask,
    sentinel_id,
    sentinel_table,
    gen_weight,
    up_weight,
    down_weight,
    cotangent,
):
    bf16, f32 = jnp.bfloat16, jnp.float32
    tok_rows, feat_width = embeddings.shape
    gen_cols = gen_weight.shape[1]
    head_count = gen_cols // KW
    head_width = feat_width // head_count
    reach = (KW - 1) // 2
    tp_count, tp_index = lax.axis_size("tp"), lax.axis_index("tp")
    sentinel_codes = jnp.arange(SENT, dtype=jnp.int32)
    onehot = sentinel_id[:, None] == sentinel_codes[None, :]
    picked = dot(onehot.astype(bf16), sentinel_table).astype(bf16)
    masked = span_mask[:, None] == 1
    hidden = jnp.where(masked, picked, embeddings)

    gen_blocks = []
    for shift in range(tp_count):
        start = (tp_index + shift) % tp_count * feat_width
        rows = lax.dynamic_slice_in_dim(gen_weight, start, feat_width, axis=0)
        gen_blocks.append(turned(rows, shift) if shift else rows)
    gen_rows = jnp.concatenate(gen_blocks, axis=1)
    partial = dot(hidden, gen_rows)
    logits = partial[:, :gen_cols]
    for shift in range(1, tp_count):
        logits = logits + turned(partial[:, shift * gen_cols : (shift + 1) * gen_cols], -shift)
    exp_logits = jnp.exp(logits)
    kernels = []
    for head in range(head_count):
        taps = exp_logits[:, head * KW : (head + 1) * KW]
        kernels.append(taps / jnp.sum(taps, axis=-1, keepdims=True))

    low, high = halo(hidden[:reach], hidden[tok_rows - reach :])
    padded = jnp.concatenate([low, hidden, high], axis=0)
    long_rows = tok_rows + 2 * reach
    ahead = jnp.arange(long_rows)[None, :] - jnp.arange(tok_rows)[:, None]
    conv = []
    for head in range(head_count):
        columns = slice(head * head_width, (head + 1) * head_width)
        band = jnp.zeros((tok_rows, long_rows), f32)
        for tap in range(KW):
            band = jnp.where(ahead == tap, kernels[head][:, tap : tap + 1], band)
        conv.append(dot(band.astype(bf16), padded[:, columns]))
    act = (hidden.astype(f32) + jnp.concatenate(conv, axis=1)).astype(bf16)

    full_cot = lax.all_gather(cotangent, "tp", axis=1, tiled=True)
    full_act = lax.all_gather(act, "tp", axis=1, tiled=True)
    middle_grad = dot(full_cot, down_weight, ((1,), (1,)))
    pre_sum = dot(full_act, up_weight)
    middle, gelu_back = jax.vjp(gelu_tanh, pre_sum)
    middle = middle.astype(bf16)
    pre_grad = gelu_back(middle_grad)[0].astype(bf16)

    back_part = dot(up_weight, pre_grad, ((1,), (1,))).astype(bf16)
    back_part, middle, pre_grad = lax.optimization_barrier((back_part, middle, pre_grad))
    act_back = lax.psum_scatter(back_part, "tp", scatter_dimension=0, tiled=True)
    down_sent, down_kept = first_halves(full_cot, middle)
    up_sent, up_kept = first_halves(full_act, pre_grad)
    down_sent, up_sent, middle, pre_grad = lax.optimization_barrier(
        (down_sent, up_sent, middle, pre_grad)
    )
    got = [swapped(block, 0) for block in down_sent + up_sent]
    kept = down_kept(middle) + up_kept(pre_grad)
    kept, middle = lax.optimization_barrier((kept, middle))
    ffn_part = dot(down_weight, middle, ((0,), (1,))).astype(bf16)
    ffn_total = lax.psum_scatter(ffn_part, "tp", scatter_dimension=0, tiled=True)
    high_bits = list(range(seq_bits() - 1, 0, -1))
    orders = [high_bits, high_bits[::-1]] * 2
    lines = [[one, two] for one, two in zip(kept, got)]
    left = [list(high_bits) for _ in lines]

    def send_all(which, step):
        return [send_parts(lines[i], left[i], orders[i][step]) for i in which]

    def swap_all(which, step, sent):
        return [swapped(block, orders[i][step]) for i, block in zip(which, sent)]

    def join_all(which, step, got):
        for i, block in zip(which, got):
            lines[i] = [keep_parts(lines[i], left[i], orders[i][step]), block]
            left[i].remove(orders[i][step])

    downs, ups = (0, 1), (2, 3)
    down_sent, up_sent = send_all(downs, 0), send_all(ups, 0)
    act_back, down_sent, up_sent = lax.optimization_barrier((act_back, down_sent, up_sent))
    down_got, up_got = swap_all(downs, 0, down_sent), swap_all(ups, 0, up_sent)
    layer_output = (act.astype(f32) + ffn_total.astype(f32).T).astype(bf16)

    act_grad = cotangent.astype(f32) + act_back.astype(f32).T
    short_grad = act_grad.astype(bf16)
    kernel_short = jnp.concatenate(kernels, axis=1).astype(bf16)
    low, high = halo(
        jnp.concatenate([short_grad[:reach], kernel_short[:reach]], axis=1),
        jnp.concatenate([short_grad[tok_rows - reach :], kernel_short[tok_rows - reach :]], axis=1),
    )
    grad_pad = jnp.concatenate([low[:, :feat_width], short_grad, high[:, :feat_width]], axis=0)
    kernel_pad = jnp.concatenate([low[:, feat_width:], kernel_short, high[:, feat_width:]], axis=0)
    taps_at = jnp.arange(gen_cols)
    kernel_grad = jnp.zeros((tok_rows, gen_cols), f32)
    for head in range(head_count):
        columns = slice(head * head_width, (head + 1) * head_width)
        scores = dot(short_grad[:, columns], padded[:, columns], ((1,), (1,)))
        for tap in range(KW):
            one = jnp.sum(jnp.where(ahead == tap, scores, 0.0), axis=-1, keepdims=True)
            kernel_grad = jnp.where(taps_at[None, :] == head * KW + tap, one, kernel_grad)
    kernel = jnp.concatenate(kernels, axis=1)
    same_head = (taps_at[:, None] // KW == taps_at[None, :] // KW).astype(f32)
    weighted = jnp.dot(kernel * kernel_grad, same_head, precision=lax.Precision.HIGHEST)
    logit_grad = (kernel * (kernel_grad - weighted)).astype(bf16)
    logit_grad, down_got = lax.optimization_barrier((logit_grad, down_got))
    join_all(downs, 0, down_got)
    down_sent = send_all(downs, 1)
    logit_grads = jnp.concatenate(
        [logit_grad] + [turned(logit_grad, shift) for shift in range(1, tp_count)], axis=1
    )

    logit_grads, up_got = lax.optimization_barrier((logit_grads, up_got))

    behind = jnp.arange(tok_rows)[None, :] - jnp.arange(long_rows)[:, None] + 2 * reach
    conv_back = []
    for head in range(head_count):
        columns = slice(head * head_width, (head + 1) * head_width)
        band = jnp.zeros((long_rows, tok_rows), f32)
        for tap in range(KW):
            place = head * KW + tap
            band = jnp.where(behind == tap, kernel_pad[:, place : place + 1].astype(f32), band)
        conv_back.append(dot(band.astype(bf16), grad_pad[:, columns], ((0,), (0,))))

    gen_part = dot(logit_grads, hidden, ((0,), (0,))).astype(bf16)
    gen_owned = [gen_part[:gen_cols]]
    for shift in range(1, tp_count):
        gen_owned.append(turned(gen_part[shift * gen_cols : (shift + 1) * gen_cols], -shift))
    gen_back = dot(logit_grads, gen_rows, ((1,), (1,)))
    hidden_grad = act_grad + jnp.concatenate(conv_back, axis=1) + gen_back
    embed_grad = jnp.where(masked, f32(0.0), hidden_grad)
    table_part = dot(
        onehot.astype(bf16), jnp.where(masked, hidden_grad, f32(0.0)).astype(bf16), ((0,), (0,))
    ).astype(bf16)
    sums = jnp.concatenate(gen_owned + [table_part], axis=0)
    join_all(ups, 0, up_got)
    up_sent = send_all(ups, 1)
    down_got = swap_all(downs, 1, down_sent)
    sums, up_sent, down_got = lax.optimization_barrier((sums, up_sent, down_got))
    up_got = swap_all(ups, 1, up_sent)
    join_all(downs, 1, down_got)
    join_all(ups, 1, up_got)
    for step in range(2, len(high_bits)):
        join_all(range(4), step, swap_all(range(4), step, send_all(range(4), step)))
    ends = [one.astype(f32) + two.astype(f32) for one, two in lines]
    down_grad = jnp.concatenate([row_major(end) for end in ends[:2]], axis=1).T
    up_grad = jnp.concatenate(ends[2:], axis=1)
    summed = seq_sum(sums)
    gen_total = tp_count * gen_cols
    table_grad = summed[gen_total:].astype(f32)
    gen_sum = summed[:gen_total].reshape(tp_count, gen_cols, feat_width)
    gen_sum = lax.dynamic_slice_in_dim(
        jnp.concatenate([gen_sum, gen_sum], axis=0), (tp_count - tp_index) % tp_count, tp_count, axis=0
    )
    gen_sum = gen_sum.transpose(0, 2, 1).reshape(tp_count * feat_width, gen_cols).astype(f32)
    return (layer_output, embed_grad, table_grad, gen_sum, up_grad, down_grad)


def solution(mesh):
    placed = (
        P("seq", "tp"),
        P("seq"),
        P("seq"),
        P(None, "tp"),
        P(None, "tp"),
        P(None, "tp"),
        P("tp", None),
        P("seq", "tp"),
    )
    return jax.shard_map(
        body,
        mesh=mesh,
        in_specs=placed,
        out_specs=(
            P("seq", "tp"),
            P("seq", "tp"),
            P(None, "tp"),
            P(None, "tp"),
            P("seq", "tp"),
            P("tp", "seq"),
        ),
        check_vma=False,
    )
```
